512 devices in a mesh: seq: 16 (over z, core), chan: 32 (over x, y).
Axes of the slice: x: 4, y: 8, z: 8, core: 2. Of those that a mesh axis runs over, the one named last changes fastest.
Arguments:
- tokens: bfloat16 [4096, 4096], P('seq', 'chan'), may hold values from -6 to 6
- w_in: bfloat16 [4096, 3, 4096], P(None, None, 'chan'), may hold values from -0.09375 to 0.09375
- filters: bfloat16 [256, 4096], P('chan'), may hold values from -0.09375 to 0.09375
- skip: float32 [4096], P('chan'), may hold values from 0.25 to 1.5
- w_out: bfloat16 [4096, 4096], P(None, 'chan'), may hold values from -0.09375 to 0.09375
Outputs:
- mixed: bfloat16 [4096, 4096], P('seq', 'chan')
The draws below stay inside these ranges and needn't reach their ends.
All inputs are finite; a program needn't handle non-finite values.
Results may differ from the reference program's by a relative error of at most 0.015.
Values may be sent and summed in bfloat16 or wider, within the bound.
No kernel may reach another device: no remote copies, remote signals or barrier semaphores. Data moves between devices by JAX's collectives and lax.ppermute only.
A program may use at most 64 MiB of HBM per device.

```python
import jax
import jax.numpy as jnp
from jax import lax

D = 4096
GSIZE = 16
TOKENS = 4096
GROUPS = 256


def level_of(rng, shape, pieces, low, top_value):
    def one(axis_at, blocks):
        heights = jax.random.uniform(jax.random.fold_in(jax.random.fold_in(rng, 6), axis_at), (blocks,), jnp.float32, low / len(pieces), top_value / len(pieces))
        return jnp.repeat(jnp.exp(heights), shape[axis_at] // blocks).reshape((-1,) + (1,) * (len(shape) - axis_at - 1))

    loudness = one(*pieces[0])
    for cut in pieces[1:]:
        loudness = loudness * one(*cut)
    return loudness


def scatter_about(stream_key, shape, deviation, bound, pieces=(), dtype=jnp.bfloat16):
    loudness = level_of(stream_key, shape, pieces, -0.22, 0.18) if pieces else 1.0
    result = jax.random.normal(stream_key, shape, jnp.float32) * deviation * loudness
    return jnp.minimum(jnp.maximum(result, -bound), bound).astype(dtype)


def setup_inputs(seed: int = 0) -> dict:
    streams_of = jax.random.split(jax.random.key(seed), 6)
    return {
        "tokens": scatter_about(streams_of[0], (TOKENS, D), 1.0, 6.0, ((0, 16), (1, 32))),
        "w_in": scatter_about(streams_of[1], (D, 3, D), D ** -0.5, 0.09375, ((2, 32),)),
        "filters": scatter_about(streams_of[2], (GROUPS, TOKENS), TOKENS ** -0.5, 0.09375, ((0, 32),)),
        "skip": jnp.clip(0.25 + 1.25 * jax.random.uniform(streams_of[3], (D,), jnp.float32) ** level_of(streams_of[3], (D,), ((0, 32),), -0.2, 0.2), 0.25, 1.5),
        "w_out": scatter_about(streams_of[4], (D, D), D ** -0.5, 0.09375, ((1, 32),)),
    }


def conv_group(args):
    values, taps = args
    size = 2 * TOKENS
    spectrum = jnp.fft.rfft(values, n=size, axis=0)
    kernel = jnp.fft.rfft(taps, n=size)
    return jnp.fft.irfft(spectrum * kernel[:, None], n=size, axis=0)[:TOKENS]


def reference(tokens, w_in, filters, skip, w_out):
    qkv = jnp.dot(tokens, w_in.reshape(D, 3 * D), preferred_element_type=jnp.float32)
    qkv = qkv.astype(jnp.bfloat16).reshape(TOKENS, 3, D)
    query = qkv[:, 0]
    source = (qkv[:, 1].astype(jnp.float32) * qkv[:, 2].astype(jnp.float32)).astype(jnp.bfloat16)
    source_f = source.astype(jnp.float32)
    grouped = source_f.reshape(TOKENS, GROUPS, GSIZE).transpose(1, 0, 2)
    convolved = lax.map(conv_group, (grouped, filters.astype(jnp.float32)))
    conv = convolved.transpose(1, 0, 2).reshape(TOKENS, D)
    gated = (query.astype(jnp.float32) * (conv + skip[None, :] * source_f)).astype(jnp.bfloat16)
    return jnp.dot(gated, w_out, preferred_element_type=jnp.float32).astype(jnp.bfloat16)
```

```python
import jax
import jax.numpy as jnp
from jax import lax
from jax.experimental import pallas as pl
from jax.experimental.pallas import tpu as pltpu
from jax.sharding import Mesh
from jax.sharding import PartitionSpec as P

GROUP = 16
LANES = 128


def vmem(*shape_and_map):
    return pl.BlockSpec(*shape_and_map, memory_space=pltpu.VMEM)


def spread(block, axis, size):
    copies = jnp.broadcast_to(block[None], (size,) + block.shape)
    return lax.all_to_all(copies, axis, 0, 0, tiled=True)


def project_kernel(x_ref, w_ref, out_ref, acc_ref):
    step = pl.program_id(0)
    left = jnp.concatenate([x_ref[i] for i in range(x_ref.shape[0])], axis=1)
    right = jnp.concatenate([w_ref[0], w_ref[1], w_ref[2]], axis=1)
    part = jnp.dot(left, right, preferred_element_type=jnp.float32)

    @pl.when(step == 0)
    def _():
        acc_ref[...] = part

    @pl.when(step > 0)
    def _():
        acc_ref[...] += part

    @pl.when(step == pl.num_programs(0) - 1)
    def _():
        chans = w_ref.shape[2]
        query, key, value = (
            acc_ref[:, i * chans : (i + 1) * chans].astype(jnp.bfloat16).astype(jnp.float32) for i in range(3)
        )
        source = (key * value).T.astype(jnp.bfloat16)
        query = query.T.astype(jnp.bfloat16)
        groups = chans // GROUP
        out_ref[:, :GROUP, :] = source.reshape(groups, GROUP, -1)
        out_ref[:, GROUP:, :] = query.reshape(groups, GROUP, -1)


def project(x, w):
    slabs, tokens, depth = x.shape
    chans = w.shape[2]
    each = slabs // 4
    return pl.pallas_call(
        project_kernel,
        grid=(4,),
        in_specs=[
            vmem((each, tokens, depth), lambda s: (s, 0, 0)),
            vmem((3, each * depth, chans), lambda s: (0, s, 0)),
        ],
        out_specs=vmem((chans // GROUP, 2 * GROUP, tokens), lambda s: (0, 0, 0)),
        out_shape=jax.ShapeDtypeStruct((chans // GROUP, 2 * GROUP, tokens), jnp.bfloat16),
        scratch_shapes=[pltpu.VMEM((tokens, 3 * chans), jnp.float32)],
        compiler_params=pltpu.CompilerParams(vmem_limit_bytes=40 * 2**20),
        name="project",
    )(x, w)


def conv_kernel(pieces_ref, filters_ref, skip_ref, out_ref, shifted_ref, strip_ref, skip_rows_ref, acc_ref):
    core, group = lax.axis_index("core"), lax.axis_index("z")
    blocks, _, block = pieces_ref.shape[1:]
    rows = blocks * GROUP
    own = pieces_ref[core]
    source = own[:, :GROUP, :].reshape(rows, block)
    query = own[:, GROUP:, :].reshape(rows, block)
    other = pieces_ref[1 - core][:, :GROUP, :].reshape(rows, block)
    shifted_ref[:GROUP, :] = jnp.zeros((GROUP, block), jnp.bfloat16)
    shifted_ref[GROUP:, :] = other
    other = shifted_ref[pl.ds(pl.multiple_of(core * GROUP, GROUP), rows), :]
    left = jnp.concatenate([source, other], axis=1)

    all_taps = filters_ref[...].astype(jnp.float32)
    mine = lax.broadcasted_iota(jnp.int32, all_taps.shape, 0) == group
    taps = jnp.sum(jnp.where(mine, all_taps, 0.0), axis=0, keepdims=True)
    length = taps.shape[1]
    padded = jnp.concatenate([jnp.zeros((1, LANES), jnp.float32), taps], axis=1)
    rolled = pltpu.roll(jnp.broadcast_to(padded, (LANES, LANES + length)), 0, 1, stride=1, stride_axis=0)
    strip_ref[:, :LANES] = jnp.zeros((LANES, LANES), jnp.bfloat16)
    strip_ref[:, LANES:] = rolled[:, LANES:].astype(jnp.bfloat16)

    for e in range(blocks):
        first = 2 * e * block
        right = jnp.concatenate(
            [
                strip_ref[:, at : at + block]
                for at in (first + LANES, first, first + block + LANES, first + block)
            ],
            axis=0,
        )
        height = rows - e * GROUP
        part = jnp.dot(left[:height], right, preferred_element_type=jnp.float32)
        if e == 0:
            acc_ref[...] = part
        else:
            acc_ref[e * GROUP :, :] += part

    skip_rows_ref[...] = jnp.broadcast_to(skip_ref[...], (LANES, LANES)).T
    skip = skip_rows_ref[pl.ds(pl.multiple_of(group * GROUP, GROUP), GROUP), :]
    skip = jnp.concatenate([skip] * (block // LANES), axis=1)
    skip = jnp.concatenate([skip] * blocks, axis=0)
    gated = query.astype(jnp.float32) * (acc_ref[...] + skip * source.astype(jnp.float32))
    out_ref[...] = gated.astype(jnp.bfloat16).reshape(out_ref.shape)


def convolve(pieces, filters, skip):
    _, blocks, _, block = pieces.shape
    rows = blocks * GROUP
    return pl.pallas_call(
        conv_kernel,
        in_specs=[vmem(), vmem(), vmem()],
        out_specs=vmem(),
        out_shape=jax.ShapeDtypeStruct((blocks, GROUP, block), jnp.bfloat16),
        scratch_shapes=[
            pltpu.VMEM((rows + GROUP, block), jnp.bfloat16),
            pltpu.VMEM((LANES, LANES + filters.shape[1]), jnp.bfloat16),
            pltpu.VMEM((LANES, LANES), jnp.float32),
            pltpu.VMEM((rows, block), jnp.float32),
        ],
        compiler_params=pltpu.CompilerParams(vmem_limit_bytes=40 * 2**20),
        name="convolve",
    )(pieces, filters, skip)


def mix_kernel(g_ref, w_ref, out_ref, acc_ref):
    step = pl.program_id(0)
    left = g_ref[...].reshape(-1, g_ref.shape[2])
    part = lax.dot_general(left, w_ref[...], (((0,), (0,)), ((), ())), preferred_element_type=jnp.float32)

    @pl.when(step == 0)
    def _():
        acc_ref[...] = part

    @pl.when(step > 0)
    def _():
        acc_ref[...] += part

    @pl.when(step == pl.num_programs(0) - 1)
    def _():
        out_ref[...] = acc_ref[...].astype(jnp.bfloat16)


def mix(gated, w):
    slabs, depth, tokens = gated.shape
    chans = w.shape[1]
    each = slabs // 4
    return pl.pallas_call(
        mix_kernel,
        grid=(4,),
        in_specs=[
            vmem((each, depth, tokens), lambda s: (s, 0, 0)),
            vmem((each * depth, chans), lambda s: (s, 0)),
        ],
        out_specs=vmem((tokens, chans), lambda s: (0, 0)),
        out_shape=jax.ShapeDtypeStruct((tokens, chans), jnp.bfloat16),
        scratch_shapes=[pltpu.VMEM((tokens, chans), jnp.float32)],
        compiler_params=pltpu.CompilerParams(vmem_limit_bytes=40 * 2**20),
        name="mix",
    )(gated, w)


def shards(tokens, w_in, filters, skip, w_out):
    def over_chan(block):
        rows = spread(block, "y", 8)
        return spread(rows, "x", 4).reshape((32,) + block.shape)

    pieces = project(over_chan(tokens), w_in.transpose(1, 0, 2))
    pieces = lax.all_to_all(pieces, "z", 0, 0, tiled=True)
    gated = convolve(lax.all_gather(pieces, "core", axis=0), filters, skip.reshape(1, -1))
    gated = lax.all_to_all(gated, "z", 0, 0, tiled=True)
    return mix(over_chan(gated.reshape(-1, gated.shape[2])), w_out)


def solution(mesh):
    fine = Mesh(mesh.devices.reshape(8, 2, 4, 8), ("z", "core", "x", "y"))
    seq, chan = ("z", "core"), ("x", "y")
    in_specs = (P(seq, chan), P(None, None, chan), P(chan, None), P(chan), P(None, chan))
    return jax.shard_map(shards, mesh=fine, in_specs=in_specs, out_specs=P(seq, chan), check_vma=False)
```

```python
import jax
import jax.numpy as jnp
from jax import lax
from jax.experimental import pallas as pl
from jax.experimental.pallas import tpu as pltpu
from jax.sharding import Mesh
from jax.sharding import PartitionSpec as P

GROUP = 16
LANES = 128
PARAMS = pltpu.CompilerParams(vmem_limit_bytes=40 * 2**20)


def vmem(*shape_and_map):
    return pl.BlockSpec(*shape_and_map, memory_space=pltpu.VMEM)


def copies(block, count):
    return jnp.broadcast_to(block[None], (count,) + block.shape)


def over_chan(blocks):
    rows = lax.all_to_all(blocks, "y_far", 0, 0, tiled=True)
    whole = lax.all_to_all(copies(rows, 8), ("x", "y_near"), 0, 0, tiled=True)
    return whole.reshape((4, 2) + rows.shape)


def project_kernel(x_ref, w_ref, out_ref):
    steps, near, far, tokens, depth = x_ref.shape
    chans = w_ref.shape[2]
    span = near * far * depth
    acc = None
    for step in range(steps):
        left = jnp.concatenate([x_ref[step, j, i] for i in range(far) for j in range(near)], axis=1)
        right = jnp.concatenate([w_ref[i, step * span : (step + 1) * span] for i in range(3)], axis=1)
        part = jnp.dot(left, right, preferred_element_type=jnp.float32)
        acc = part if acc is None else acc + part
    query, key, value = (
        acc[:, i * chans : (i + 1) * chans].astype(jnp.bfloat16).astype(jnp.float32) for i in range(3)
    )
    groups = chans // GROUP
    out_ref[:, :GROUP, :] = (key * value).T.astype(jnp.bfloat16).reshape(groups, GROUP, -1)
    out_ref[:, GROUP:, :] = query.T.astype(jnp.bfloat16).reshape(groups, GROUP, -1)


def project(x, w):
    tokens, chans = x.shape[3], w.shape[2]
    return pl.pallas_call(
        project_kernel,
        in_specs=[vmem(), vmem()],
        out_specs=vmem(),
        out_shape=jax.ShapeDtypeStruct((chans // GROUP, 2 * GROUP, tokens), jnp.bfloat16),
        compiler_params=PARAMS,
        name="project",
    )(x, w)


def conv_kernel(pieces_ref, filters_ref, skip_ref, out_ref, shifted_ref, strip_ref, skip_rows_ref, acc_ref):
    core, group = lax.axis_index("core"), lax.axis_index("z")
    blocks, _, block = pieces_ref.shape[1:]
    rows = blocks * GROUP
    own = pieces_ref[core]
    source = own[:, :GROUP, :].reshape(rows, block)
    query = own[:, GROUP:, :].reshape(rows, block)
    other = pieces_ref[1 - core][:, :GROUP, :].reshape(rows, block)
    shifted_ref[:GROUP, :] = jnp.zeros((GROUP, block), jnp.bfloat16)
    shifted_ref[GROUP:, :] = other
    other = shifted_ref[pl.ds(pl.multiple_of(core * GROUP, GROUP), rows), :]
    left = jnp.concatenate([source, other], axis=1)

    all_taps = filters_ref[...].astype(jnp.float32)
    mine = lax.broadcasted_iota(jnp.int32, all_taps.shape, 0) == group
    taps = jnp.sum(jnp.where(mine, all_taps, 0.0), axis=0, keepdims=True)
    length = taps.shape[1]
    padded = jnp.concatenate([jnp.zeros((1, LANES), jnp.float32), taps], axis=1)
    rolled = pltpu.roll(jnp.broadcast_to(padded, (LANES, LANES + length)), 0, 1, stride=1, stride_axis=0)
    strip_ref[:, :LANES] = jnp.zeros((LANES, LANES), jnp.bfloat16)
    strip_ref[:, LANES:] = rolled[:, LANES:].astype(jnp.bfloat16)

    for e in range(blocks):
        first = 2 * e * block
        right = jnp.concatenate(
            [
                strip_ref[:, at : at + block]
                for at in (first + LANES, first, first + block + LANES, first + block)
            ],
            axis=0,
        )
        height = rows - e * GROUP
        part = jnp.dot(left[:height], right, preferred_element_type=jnp.float32)
        if e == 0:
            acc_ref[...] = part
        else:
            acc_ref[e * GROUP :, :] += part

    skip_rows_ref[...] = jnp.broadcast_to(skip_ref[...], (LANES, LANES)).T
    skip = skip_rows_ref[pl.ds(pl.multiple_of(group * GROUP, GROUP), GROUP), :]
    skip = jnp.concatenate([skip] * (block // LANES), axis=1)
    skip = jnp.concatenate([skip] * blocks, axis=0)
    gated = query.astype(jnp.float32) * (acc_ref[...] + skip * source.astype(jnp.float32))
    out_ref[...] = gated.astype(jnp.bfloat16).reshape(out_ref.shape)


def convolve(pieces, filters, skip):
    _, blocks, _, block = pieces.shape
    rows = blocks * GROUP
    return pl.pallas_call(
        conv_kernel,
        in_specs=[vmem(), vmem(), vmem()],
        out_specs=vmem(),
        out_shape=jax.ShapeDtypeStruct((blocks, GROUP, block), jnp.bfloat16),
        scratch_shapes=[
            pltpu.VMEM((rows + GROUP, block), jnp.bfloat16),
            pltpu.VMEM((LANES, LANES + filters.shape[1]), jnp.bfloat16),
            pltpu.VMEM((LANES, LANES), jnp.float32),
            pltpu.VMEM((rows, block), jnp.float32),
        ],
        compiler_params=PARAMS,
        name="convolve",
    )(pieces, filters, skip)


def turn_kernel(g_ref, out_ref):
    turned = g_ref[...].astype(jnp.float32).reshape(-1, g_ref.shape[2]).T.astype(jnp.bfloat16)
    for i in range(out_ref.shape[0]):
        out_ref[i] = turned


def turn(gated, copies):
    sources, rows, tokens = gated.shape
    return pl.pallas_call(
        turn_kernel,
        in_specs=[vmem()],
        out_specs=vmem(),
        out_shape=jax.ShapeDtypeStruct((copies, tokens, sources * rows), jnp.bfloat16),
        compiler_params=PARAMS,
        name="turn",
    )(gated)


def mix_kernel(g_ref, w_ref, out_ref):
    steps, near, far, tokens, depth = g_ref.shape
    span = near * far * depth
    acc = None
    for step in range(steps):
        left = jnp.concatenate([g_ref[step, j, i] for i in range(far) for j in range(near)], axis=1)
        part = jnp.dot(left, w_ref[step * span : (step + 1) * span], preferred_element_type=jnp.float32)
        acc = part if acc is None else acc + part
    out_ref[...] = acc.astype(jnp.bfloat16)


def mix(gated, w):
    return pl.pallas_call(
        mix_kernel,
        in_specs=[vmem(), vmem()],
        out_specs=vmem(),
        out_shape=jax.ShapeDtypeStruct((gated.shape[3], w.shape[1]), jnp.bfloat16),
        compiler_params=PARAMS,
        name="mix",
    )(gated, w)


def shards(tokens, w_in, filters, skip, w_out):
    pieces = project(over_chan(copies(tokens, 4)), w_in.transpose(1, 0, 2))
    pieces = lax.all_to_all(pieces, "z", 0, 0, tiled=True)
    gated = convolve(lax.all_gather(pieces, "core", axis=0), filters, skip.reshape(1, -1))
    gated = lax.all_to_all(gated, "z", 0, 0, tiled=True)
    return mix(over_chan(turn(gated, 4)), w_out)


def solution(mesh):
    fine = Mesh(mesh.devices.reshape(8, 2, 4, 4, 2), ("z", "core", "x", "y_far", "y_near"))
    seq, chan = ("z", "core"), ("x", "y_far", "y_near")
    in_specs = (P(seq, chan), P(None, None, chan), P(chan, None), P(chan), P(None, chan))
    return jax.shard_map(shards, mesh=fine, in_specs=in_specs, out_specs=P(seq, chan), check_vma=False)
```

```python
import jax
import jax.numpy as jnp
from jax import lax
from jax.experimental import pallas as pl
from jax.experimental.pallas import tpu as pltpu
from jax.sharding import Mesh
from jax.sharding import PartitionSpec as P

GROUP = 16
LANES = 128
PARAMS = pltpu.CompilerParams(vmem_limit_bytes=40 * 2**20)


def vmem(*shape_and_map):
    return pl.BlockSpec(*shape_and_map, memory_space=pltpu.VMEM)


def pack_kernel(x_ref, w_ref, out_ref):
    core = lax.axis_index("core")
    far, tokens, _ = x_ref.shape
    depth = w_ref.shape[1]
    half = far // 2
    x = x_ref[...].reshape(far * tokens, -1)
    for peer in range(out_ref.shape[0]):
        out_ref[peer, : far * tokens] = x
        for i in range(half):
            slab = peer // 2 * 2 * far + (half * core + i) * 2 + peer % 2
            at = far * tokens + i * depth
            out_ref[peer, at : at + depth] = w_ref[slab]


def pack(x, w, peers):
    far, tokens, depth = x.shape
    rows = w.shape[0] // (2 * peers)
    return pl.pallas_call(
        pack_kernel,
        in_specs=[vmem(), vmem()],
        out_specs=vmem(),
        out_shape=jax.ShapeDtypeStruct((peers, far * tokens + rows, depth), x.dtype),
        compiler_params=PARAMS,
        name="pack",
    )(x, w.reshape(-1, depth, w.shape[1]))


def project_kernel(x_ref, w_ref, out_ref, rows_ref):
    depth, chans = x_ref.shape[2], w_ref.shape[2]
    tokens = out_ref.shape[2]
    far = w_ref.shape[1] // (x_ref.shape[0] * depth)
    span = 2 * far * depth
    rows_ref[...] = x_ref[:, far * tokens :]
    acc = None
    for step in range(x_ref.shape[0] // 2):
        left = jnp.concatenate(
            [x_ref[2 * step + j, i * tokens : (i + 1) * tokens] for i in range(far) for j in range(2)], axis=1
        )
        right = jnp.concatenate([w_ref[i, step * span : (step + 1) * span] for i in range(3)], axis=1)
        part = jnp.dot(left, right, preferred_element_type=jnp.float32)
        acc = part if acc is None else acc + part
    query, key, value = (
        acc[:, i * chans : (i + 1) * chans].astype(jnp.bfloat16).astype(jnp.float32) for i in range(3)
    )
    groups = chans // GROUP
    out_ref[:, :GROUP, :] = (key * value).T.astype(jnp.bfloat16).reshape(groups, GROUP, -1)
    out_ref[:, GROUP:, :] = query.T.astype(jnp.bfloat16).reshape(groups, GROUP, -1)


def project(x, w, tokens):
    chans = w.shape[2]
    rows = x.shape[1] - w.shape[1] // (x.shape[0] * x.shape[2]) * tokens
    return pl.pallas_call(
        project_kernel,
        in_specs=[vmem(), vmem()],
        out_specs=[vmem(), vmem()],
        out_shape=[
            jax.ShapeDtypeStruct((chans // GROUP, 2 * GROUP, tokens), jnp.bfloat16),
            jax.ShapeDtypeStruct((x.shape[0], rows, x.shape[2]), jnp.bfloat16),
        ],
        compiler_params=PARAMS,
        name="project",
    )(x, w)


def conv_kernel(pieces_ref, filters_ref, skip_ref, out_ref, shifted_ref, strip_ref, skip_rows_ref, acc_ref):
    core, group = lax.axis_index("core"), lax.axis_index("z")
    blocks, _, block = pieces_ref.shape[1:]
    rows = blocks * GROUP
    own = pieces_ref[core]
    source = own[:, :GROUP, :].reshape(rows, block)
    query = own[:, GROUP:, :].reshape(rows, block)
    other = pieces_ref[1 - core][:, :GROUP, :].reshape(rows, block)
    shifted_ref[:GROUP, :] = jnp.zeros((GROUP, block), jnp.bfloat16)
    shifted_ref[GROUP:, :] = other
    other = shifted_ref[pl.ds(pl.multiple_of(core * GROUP, GROUP), rows), :]
    left = jnp.concatenate([source, other], axis=1)

    all_taps = filters_ref[...].astype(jnp.float32)
    mine = lax.broadcasted_iota(jnp.int32, all_taps.shape, 0) == group
    taps = jnp.sum(jnp.where(mine, all_taps, 0.0), axis=0, keepdims=True)
    length = taps.shape[1]
    padded = jnp.concatenate([jnp.zeros((1, LANES), jnp.float32), taps], axis=1)
    rolled = pltpu.roll(jnp.broadcast_to(padded, (LANES, LANES + length)), 0, 1, stride=1, stride_axis=0)
    strip_ref[:, :LANES] = jnp.zeros((LANES, LANES), jnp.bfloat16)
    strip_ref[:, LANES:] = rolled[:, LANES:].astype(jnp.bfloat16)

    for e in range(blocks):
        first = 2 * e * block
        right = jnp.concatenate(
            [
                strip_ref[:, at : at + block]
                for at in (first + LANES, first, first + block + LANES, first + block)
            ],
            axis=0,
        )
        height = rows - e * GROUP
        part = jnp.dot(left[:height], right, preferred_element_type=jnp.float32)
        if e == 0:
            acc_ref[...] = part
        else:
            acc_ref[e * GROUP :, :] += part

    skip_rows_ref[...] = jnp.broadcast_to(skip_ref[...], (LANES, LANES)).T
    skip = skip_rows_ref[pl.ds(pl.multiple_of(group * GROUP, GROUP), GROUP), :]
    skip = jnp.concatenate([skip] * (block // LANES), axis=1)
    skip = jnp.concatenate([skip] * blocks, axis=0)
    gated = query.astype(jnp.float32) * (acc_ref[...] + skip * source.astype(jnp.float32))
    gated = gated.astype(jnp.bfloat16).reshape(out_ref.shape[1:])
    for i in range(out_ref.shape[0]):
        out_ref[i] = gated


def convolve(pieces, filters, skip, count):
    _, blocks, _, block = pieces.shape
    rows = blocks * GROUP
    return pl.pallas_call(
        conv_kernel,
        in_specs=[vmem(), vmem(), vmem()],
        out_specs=vmem(),
        out_shape=jax.ShapeDtypeStruct((count, blocks, GROUP, block), jnp.bfloat16),
        scratch_shapes=[
            pltpu.VMEM((rows + GROUP, block), jnp.bfloat16),
            pltpu.VMEM((LANES, LANES + filters.shape[1]), jnp.bfloat16),
            pltpu.VMEM((LANES, LANES), jnp.float32),
            pltpu.VMEM((rows, block), jnp.float32),
        ],
        compiler_params=PARAMS,
        name="convolve",
    )(pieces, filters, skip)


def mix_kernel(g_ref, own_ref, other_ref, out_ref, turned_ref):
    core = lax.axis_index("core")
    far, _, _, tokens = g_ref.shape
    peers, rows, chans = own_ref.shape
    for i in range(far):
        turned_ref[i] = g_ref[i].astype(jnp.float32).reshape(-1, tokens).T.astype(jnp.bfloat16)
    half = far // 2
    acc = None
    for w_ref, at in ((own_ref, core), (other_ref, 1 - core)):
        left = jnp.concatenate([turned_ref[half * at + i] for i in range(half)], axis=1)
        right = jnp.concatenate([w_ref[peer] for peer in range(peers)], axis=1)
        part = jnp.dot(left, right, preferred_element_type=jnp.float32)
        acc = part if acc is None else acc + part
    for peer in range(peers):
        out_ref[peer] = acc[:, peer * chans : (peer + 1) * chans].astype(jnp.bfloat16)


def mix(gated, own, other):
    far, groups, rows, tokens = gated.shape
    peers, _, chans = own.shape
    return pl.pallas_call(
        mix_kernel,
        in_specs=[vmem(), vmem(), vmem()],
        out_specs=vmem(),
        out_shape=jax.ShapeDtypeStruct((peers, tokens, chans), jnp.bfloat16),
        scratch_shapes=[pltpu.VMEM((far, tokens, groups * rows), jnp.bfloat16)],
        compiler_params=PARAMS,
        name="mix",
    )(gated, own, other)


def add_kernel(parts_ref, out_ref):
    total = parts_ref[0].astype(jnp.float32)
    for i in range(1, parts_ref.shape[0]):
        total += parts_ref[i].astype(jnp.float32)
    out_ref[...] = total.astype(jnp.bfloat16)


def add(parts):
    return pl.pallas_call(
        add_kernel,
        in_specs=[vmem()],
        out_specs=vmem(),
        out_shape=jax.ShapeDtypeStruct(parts.shape[1:], jnp.bfloat16),
        compiler_params=PARAMS,
        name="add",
    )(parts)


def shards(tokens, w_in, filters, skip, w_out):
    near = ("x", "y_near")
    x = lax.all_gather(tokens, "y_far", axis=0)
    x = lax.all_to_all(pack(x, w_out, 8), near, 0, 0, tiled=True)
    pieces, own = project(x, w_in.transpose(1, 0, 2), tokens.shape[0])
    other = lax.ppermute(own, "core", [(0, 1), (1, 0)])
    pieces = lax.all_to_all(pieces, "z", 0, 0, tiled=True)
    gated = convolve(lax.all_gather(pieces, "core", axis=0), filters, skip.reshape(1, -1), 4)
    shape = gated.shape
    gated = lax.all_to_all(gated.reshape((-1,) + shape[2:]), ("y_far", "z"), 0, 0, tiled=True)
    parts = mix(gated.reshape(shape), own, other)
    return add(lax.all_to_all(parts, near, 0, 0, tiled=True))


def solution(mesh):
    fine = Mesh(mesh.devices.reshape(8, 2, 4, 4, 2), ("z", "core", "x", "y_far", "y_near"))
    seq, chan = ("z", "core"), ("x", "y_far", "y_near")
    in_specs = (P(seq, chan), P(None, None, chan), P(chan, None), P(chan), P(None, chan))
    return jax.shard_map(shards, mesh=fine, in_specs=in_specs, out_specs=P(seq, chan), check_vma=False)
```

```python
import jax
import jax.numpy as jnp
from jax import lax
from jax.experimental import pallas as pl
from jax.experimental.pallas import tpu as pltpu
from jax.sharding import Mesh
from jax.sharding import PartitionSpec as P

GROUP = 16
LANES = 128
PARAMS = pltpu.CompilerParams(vmem_limit_bytes=40 * 2**20)


def vmem(*shape_and_map):
    return pl.BlockSpec(*shape_and_map, memory_space=pltpu.VMEM)


def pack_kernel(x_ref, w_ref, out_ref):
    far, tokens, _ = x_ref.shape
    depth = w_ref.shape[1]
    mine = 2 * lax.axis_index("core") + lax.rem(lax.axis_index("z"), 2)
    x = x_ref[...].reshape(far * tokens, -1)
    for peer in range(out_ref.shape[0]):
        out_ref[peer, : far * tokens] = x
        out_ref[peer, far * tokens :] = w_ref[(peer // 2 * far + mine) * 2 + peer % 2]


def pack(x, w, peers):
    far, tokens, depth = x.shape
    return pl.pallas_call(
        pack_kernel,
        in_specs=[vmem(), vmem()],
        out_specs=vmem(),
        out_shape=jax.ShapeDtypeStruct((peers, far * tokens + depth, depth), x.dtype),
        compiler_params=PARAMS,
        name="pack",
    )(x, w.reshape(-1, depth, w.shape[1]))


def project_kernel(x_ref, w_ref, out_ref, rows_ref):
    depth, chans = x_ref.shape[2], w_ref.shape[2]
    tokens = out_ref.shape[2]
    far = w_ref.shape[1] // (x_ref.shape[0] * depth)
    span = 2 * far * depth
    rows_ref[...] = x_ref[:, far * tokens :]
    acc = None
    for step in range(x_ref.shape[0] // 2):
        left = jnp.concatenate(
            [x_ref[2 * step + j, i * tokens : (i + 1) * tokens] for i in range(far) for j in range(2)], axis=1
        )
        right = jnp.concatenate([w_ref[i, step * span : (step + 1) * span] for i in range(3)], axis=1)
        part = jnp.dot(left, right, preferred_element_type=jnp.float32)
        acc = part if acc is None else acc + part
    query, key, value = (
        acc[:, i * chans : (i + 1) * chans].astype(jnp.bfloat16).astype(jnp.float32) for i in range(3)
    )
    groups = chans // GROUP
    out_ref[:, :GROUP, :] = (key * value).T.astype(jnp.bfloat16).reshape(groups, GROUP, -1)
    out_ref[:, GROUP:, :] = query.T.astype(jnp.bfloat16).reshape(groups, GROUP, -1)


def project(x, w, tokens):
    chans = w.shape[2]
    rows = x.shape[1] - w.shape[1] // (x.shape[0] * x.shape[2]) * tokens
    return pl.pallas_call(
        project_kernel,
        in_specs=[vmem(), vmem()],
        out_specs=[vmem(), vmem()],
        out_shape=[
            jax.ShapeDtypeStruct((chans // GROUP, 2 * GROUP, tokens), jnp.bfloat16),
            jax.ShapeDtypeStruct((x.shape[0], rows, x.shape[2]), jnp.bfloat16),
        ],
        compiler_params=PARAMS,
        name="project",
    )(x, w)


def conv_kernel(pieces_ref, filters_ref, skip_ref, out_ref, shifted_ref, strip_ref, skip_rows_ref, acc_ref):
    core, group = lax.axis_index("core"), lax.axis_index("z")
    blocks, _, block = pieces_ref.shape[1:]
    rows = blocks * GROUP
    own = pieces_ref[core]
    source = own[:, :GROUP, :].reshape(rows, block)
    query = own[:, GROUP:, :].reshape(rows, block)
    other = pieces_ref[1 - core][:, :GROUP, :].reshape(rows, block)
    shifted_ref[:GROUP, :] = jnp.zeros((GROUP, block), jnp.bfloat16)
    shifted_ref[GROUP:, :] = other
    other = shifted_ref[pl.ds(pl.multiple_of(core * GROUP, GROUP), rows), :]
    left = jnp.concatenate([source, other], axis=1)

    all_taps = filters_ref[...].astype(jnp.float32)
    mine = lax.broadcasted_iota(jnp.int32, all_taps.shape, 0) == group
    taps = jnp.sum(jnp.where(mine, all_taps, 0.0), axis=0, keepdims=True)
    length = taps.shape[1]
    padded = jnp.concatenate([jnp.zeros((1, LANES), jnp.float32), taps], axis=1)
    rolled = pltpu.roll(jnp.broadcast_to(padded, (LANES, LANES + length)), 0, 1, stride=1, stride_axis=0)
    strip_ref[:, :LANES] = jnp.zeros((LANES, LANES), jnp.bfloat16)
    strip_ref[:, LANES:] = rolled[:, LANES:].astype(jnp.bfloat16)

    for e in range(blocks):
        first = 2 * e * block
        right = jnp.concatenate(
            [
                strip_ref[:, at : at + block]
                for at in (first + LANES, first, first + block + LANES, first + block)
            ],
            axis=0,
        )
        height = rows - e * GROUP
        part = jnp.dot(left[:height], right, preferred_element_type=jnp.float32)
        if e == 0:
            acc_ref[...] = part
        else:
            acc_ref[e * GROUP :, :] += part

    skip_rows_ref[...] = jnp.broadcast_to(skip_ref[...], (LANES, LANES)).T
    skip = skip_rows_ref[pl.ds(pl.multiple_of(group * GROUP, GROUP), GROUP), :]
    skip = jnp.concatenate([skip] * (block // LANES), axis=1)
    skip = jnp.concatenate([skip] * blocks, axis=0)
    gated = query.astype(jnp.float32) * (acc_ref[...] + skip * source.astype(jnp.float32))
    gated = gated.astype(jnp.bfloat16).reshape(out_ref.shape[1:])
    for i in range(out_ref.shape[0]):
        out_ref[i] = gated


def convolve(pieces, filters, skip, count):
    _, blocks, _, block = pieces.shape
    rows = blocks * GROUP
    return pl.pallas_call(
        conv_kernel,
        in_specs=[vmem(), vmem(), vmem()],
        out_specs=vmem(),
        out_shape=jax.ShapeDtypeStruct((count, blocks, GROUP, block), jnp.bfloat16),
        scratch_shapes=[
            pltpu.VMEM((rows + GROUP, block), jnp.bfloat16),
            pltpu.VMEM((LANES, LANES + filters.shape[1]), jnp.bfloat16),
            pltpu.VMEM((LANES, LANES), jnp.float32),
            pltpu.VMEM((rows, block), jnp.float32),
        ],
        compiler_params=PARAMS,
        name="convolve",
    )(pieces, filters, skip)


def mix_kernel(g_ref, *refs):
    w_refs, out_ref, turned_ref = refs[:-2], refs[-2], refs[-1]
    core, odd = lax.axis_index("core"), lax.rem(lax.axis_index("z"), 2)
    far, _, _, tokens = g_ref.shape
    peers, _, chans = w_refs[0].shape
    for i in range(far):
        turned_ref[i] = g_ref[i].astype(jnp.float32).reshape(-1, tokens).T.astype(jnp.bfloat16)
    acc = None
    for pair, at in ((w_refs[:2], core), (w_refs[2:], 1 - core)):
        left = jnp.concatenate([turned_ref[2 * at + odd], turned_ref[2 * at + 1 - odd]], axis=1)
        right = jnp.concatenate(
            [jnp.concatenate([w_ref[peer] for w_ref in pair], axis=0) for peer in range(peers)], axis=1
        )
        part = jnp.dot(left, right, preferred_element_type=jnp.float32)
        acc = part if acc is None else acc + part
    for peer in range(peers):
        out_ref[peer] = acc[:, peer * chans : (peer + 1) * chans].astype(jnp.bfloat16)


def mix(gated, *w):
    far, groups, rows, tokens = gated.shape
    peers, _, chans = w[0].shape
    return pl.pallas_call(
        mix_kernel,
        in_specs=[vmem()] * (1 + len(w)),
        out_specs=vmem(),
        out_shape=jax.ShapeDtypeStruct((peers, tokens, chans), jnp.bfloat16),
        scratch_shapes=[pltpu.VMEM((far, tokens, groups * rows), jnp.bfloat16)],
        compiler_params=PARAMS,
        name="mix",
    )(gated, *w)


def add_kernel(parts_ref, out_ref):
    total = parts_ref[0].astype(jnp.float32)
    for i in range(1, parts_ref.shape[0]):
        total += parts_ref[i].astype(jnp.float32)
    out_ref[...] = total.astype(jnp.bfloat16)


def add(parts):
    return pl.pallas_call(
        add_kernel,
        in_specs=[vmem()],
        out_specs=vmem(),
        out_shape=jax.ShapeDtypeStruct(parts.shape[1:], jnp.bfloat16),
        compiler_params=PARAMS,
        name="add",
    )(parts)


def shards(tokens, w_in, filters, skip, w_out):
    near = ("x", "y_near")
    x = lax.all_gather(tokens, "y_far", axis=0)
    x = lax.all_to_all(pack(x, w_out, 8), near, 0, 0, tiled=True)
    pieces, own = project(x, w_in.transpose(1, 0, 2), tokens.shape[0])
    beside = lax.ppermute(own, "z", [(i, i ^ 1) for i in range(8)])
    pieces = lax.all_to_all(pieces, "z", 0, 0, tiled=True)
    gated = convolve(lax.all_gather(pieces, "core", axis=0), filters, skip.reshape(1, -1), 4)
    others = [lax.ppermute(rows, "core", [(0, 1), (1, 0)]) for rows in (own, beside)]
    shape = gated.shape
    gated = lax.all_to_all(gated.reshape((-1,) + shape[2:]), ("y_far", "z"), 0, 0, tiled=True)
    parts = mix(gated.reshape(shape), own, beside, *others)
    return add(lax.all_to_all(parts, near, 0, 0, tiled=True))


def solution(mesh):
    fine = Mesh(mesh.devices.reshape(8, 2, 4, 4, 2), ("z", "core", "x", "y_far", "y_near"))
    seq, chan = ("z", "core"), ("x", "y_far", "y_near")
    in_specs = (P(seq, chan), P(None, None, chan), P(chan, None), P(chan), P(None, chan))
    return jax.shard_map(shards, mesh=fine, in_specs=in_specs, out_specs=P(seq, chan), check_vma=False)
```

```python
import jax
import jax.numpy as jnp
from jax import lax
from jax.experimental import pallas as pl
from jax.experimental.pallas import tpu as pltpu
from jax.sharding import Mesh
from jax.sharding import PartitionSpec as P

GROUP = 16
LANES = 128
PARAMS = pltpu.CompilerParams(vmem_limit_bytes=40 * 2**20)


def vmem(*shape_and_map):
    return pl.BlockSpec(*shape_and_map, memory_space=pltpu.VMEM)


def pack_kernel(x_ref, w_hbm, out_ref, sems):
    far, tokens, _ = x_ref.shape
    depth = w_hbm.shape[1]
    mine = 2 * lax.axis_index("core") + lax.rem(lax.axis_index("z"), 2)
    sends = [
        pltpu.make_async_copy(
            w_hbm.at[(peer // 2 * far + mine) * 2 + peer % 2],
            out_ref.at[peer, pl.ds(far * tokens, depth)],
            sems.at[peer],
        )
        for peer in range(out_ref.shape[0])
    ]
    for send in sends:
        send.start()
    x = x_ref[...].reshape(far * tokens, -1)
    for peer in range(out_ref.shape[0]):
        out_ref[peer, : far * tokens] = x
    for send in sends:
        send.wait()


def pack(x, w, peers):
    far, tokens, depth = x.shape
    w = pltpu.with_memory_space_constraint(w.reshape(-1, depth, w.shape[1]), pltpu.HBM)
    return pl.pallas_call(
        pack_kernel,
        in_specs=[vmem(), pl.BlockSpec(memory_space=pltpu.HBM)],
        out_specs=vmem(),
        out_shape=jax.ShapeDtypeStruct((peers, far * tokens + depth, depth), x.dtype),
        scratch_shapes=[pltpu.SemaphoreType.DMA((peers,))],
        compiler_params=PARAMS,
        name="pack",
    )(x, w)


def project_kernel(x_ref, w_ref, out_ref, rows_ref):
    depth, chans = x_ref.shape[2], w_ref.shape[2]
    tokens = out_ref.shape[2]
    far = w_ref.shape[1] // (x_ref.shape[0] * depth)
    span = 2 * far * depth
    rows_ref[...] = x_ref[:, far * tokens :]
    acc = None
    for step in range(x_ref.shape[0] // 2):
        left = jnp.concatenate(
            [x_ref[2 * step + j, i * tokens : (i + 1) * tokens] for i in range(far) for j in range(2)], axis=1
        )
        right = jnp.concatenate([w_ref[i, step * span : (step + 1) * span] for i in range(3)], axis=1)
        part = jnp.dot(left, right, preferred_element_type=jnp.float32)
        acc = part if acc is None else acc + part
    query, key, value = (
        acc[:, i * chans : (i + 1) * chans].astype(jnp.bfloat16).astype(jnp.float32) for i in range(3)
    )
    groups = chans // GROUP
    out_ref[:, :GROUP, :] = (key * value).T.astype(jnp.bfloat16).reshape(groups, GROUP, -1)
    out_ref[:, GROUP:, :] = query.T.astype(jnp.bfloat16).reshape(groups, GROUP, -1)


def project(x, w, tokens):
    chans = w.shape[2]
    rows = x.shape[1] - w.shape[1] // (x.shape[0] * x.shape[2]) * tokens
    return pl.pallas_call(
        project_kernel,
        in_specs=[vmem(), vmem()],
        out_specs=[vmem(), vmem()],
        out_shape=[
            jax.ShapeDtypeStruct((chans // GROUP, 2 * GROUP, tokens), jnp.bfloat16),
            jax.ShapeDtypeStruct((x.shape[0], rows, x.shape[2]), jnp.bfloat16),
        ],
        compiler_params=PARAMS,
        name="project",
    )(x, w)


def conv_kernel(pieces_ref, filters_ref, skip_ref, out_ref, shifted_ref, strip_ref, skip_rows_ref, acc_ref):
    core, group = lax.axis_index("core"), lax.axis_index("z")
    blocks, _, block = pieces_ref.shape[1:]
    rows = blocks * GROUP
    own = pieces_ref[core]
    source = own[:, :GROUP, :].reshape(rows, block)
    query = own[:, GROUP:, :].reshape(rows, block)
    other = pieces_ref[1 - core][:, :GROUP, :].reshape(rows, block)
    shifted_ref[:GROUP, :] = jnp.zeros((GROUP, block), jnp.bfloat16)
    shifted_ref[GROUP:, :] = other
    other = shifted_ref[pl.ds(pl.multiple_of(core * GROUP, GROUP), rows), :]
    left = jnp.concatenate([source, other], axis=1)

    all_taps = filters_ref[...].astype(jnp.float32)
    mine = lax.broadcasted_iota(jnp.int32, all_taps.shape, 0) == group
    taps = jnp.sum(jnp.where(mine, all_taps, 0.0), axis=0, keepdims=True)
    length = taps.shape[1]
    padded = jnp.concatenate([jnp.zeros((1, LANES), jnp.float32), taps], axis=1)
    rolled = pltpu.roll(jnp.broadcast_to(padded, (LANES, LANES + length)), 0, 1, stride=1, stride_axis=0)
    strip_ref[:, :LANES] = jnp.zeros((LANES, LANES), jnp.bfloat16)
    strip_ref[:, LANES:] = rolled[:, LANES:].astype(jnp.bfloat16)

    for e in range(blocks):
        first = 2 * e * block
        right = jnp.concatenate(
            [
                strip_ref[:, at : at + block]
                for at in (first + LANES, first, first + block + LANES, first + block)
            ],
            axis=0,
        )
        height = rows - e * GROUP
        part = jnp.dot(left[:height], right, preferred_element_type=jnp.float32)
        if e == 0:
            acc_ref[...] = part
        else:
            acc_ref[e * GROUP :, :] += part

    skip_rows_ref[...] = jnp.broadcast_to(skip_ref[...], (LANES, LANES)).T
    skip = skip_rows_ref[pl.ds(pl.multiple_of(group * GROUP, GROUP), GROUP), :]
    skip = jnp.concatenate([skip] * (block // LANES), axis=1)
    skip = jnp.concatenate([skip] * blocks, axis=0)
    gated = query.astype(jnp.float32) * (acc_ref[...] + skip * source.astype(jnp.float32))
    gated = gated.astype(jnp.bfloat16).reshape(out_ref.shape[1:])
    for i in range(out_ref.shape[0]):
        out_ref[i] = gated


def convolve(pieces, filters, skip, count):
    _, blocks, _, block = pieces.shape
    rows = blocks * GROUP
    return pl.pallas_call(
        conv_kernel,
        in_specs=[vmem(), vmem(), vmem()],
        out_specs=vmem(),
        out_shape=jax.ShapeDtypeStruct((count, blocks, GROUP, block), jnp.bfloat16),
        scratch_shapes=[
            pltpu.VMEM((rows + GROUP, block), jnp.bfloat16),
            pltpu.VMEM((LANES, LANES + filters.shape[1]), jnp.bfloat16),
            pltpu.VMEM((LANES, LANES), jnp.float32),
            pltpu.VMEM((rows, block), jnp.float32),
        ],
        compiler_params=PARAMS,
        name="convolve",
    )(pieces, filters, skip)


def mix_kernel(g_ref, *refs):
    w_refs, out_ref, turned_ref = refs[:-2], refs[-2], refs[-1]
    core, odd = lax.axis_index("core"), lax.rem(lax.axis_index("z"), 2)
    far, _, _, tokens = g_ref.shape
    peers, _, chans = w_refs[0].shape
    for i in range(far):
        turned_ref[i] = g_ref[i].astype(jnp.float32).reshape(-1, tokens).T.astype(jnp.bfloat16)
    acc = None
    for pair, at in ((w_refs[:2], core), (w_refs[2:], 1 - core)):
        left = jnp.concatenate([turned_ref[2 * at + odd], turned_ref[2 * at + 1 - odd]], axis=1)
        right = jnp.concatenate(
            [jnp.concatenate([w_ref[peer] for w_ref in pair], axis=0) for peer in range(peers)], axis=1
        )
        part = jnp.dot(left, right, preferred_element_type=jnp.float32)
        acc = part if acc is None else acc + part
    for peer in range(peers):
        out_ref[peer] = acc[:, peer * chans : (peer + 1) * chans].astype(jnp.bfloat16)


def mix(gated, *w):
    far, groups, rows, tokens = gated.shape
    peers, _, chans = w[0].shape
    return pl.pallas_call(
        mix_kernel,
        in_specs=[vmem()] * (1 + len(w)),
        out_specs=vmem(),
        out_shape=jax.ShapeDtypeStruct((peers, tokens, chans), jnp.bfloat16),
        scratch_shapes=[pltpu.VMEM((far, tokens, groups * rows), jnp.bfloat16)],
        compiler_params=PARAMS,
        name="mix",
    )(gated, *w)


def add_kernel(parts_ref, out_ref):
    total = parts_ref[0].astype(jnp.float32)
    for i in range(1, parts_ref.shape[0]):
        total += parts_ref[i].astype(jnp.float32)
    out_ref[...] = total.astype(jnp.bfloat16)


def add(parts):
    return pl.pallas_call(
        add_kernel,
        in_specs=[vmem()],
        out_specs=vmem(),
        out_shape=jax.ShapeDtypeStruct(parts.shape[1:], jnp.bfloat16),
        compiler_params=PARAMS,
        name="add",
    )(parts)


def shards(tokens, w_in, filters, skip, w_out):
    near = ("x", "y_near")
    x = lax.all_gather(tokens, "y_far", axis=0)
    x = lax.all_to_all(pack(x, w_out, 8), near, 0, 0, tiled=True)
    pieces, own = project(x, w_in.transpose(1, 0, 2), tokens.shape[0])
    beside = lax.ppermute(own, "z", [(i, i ^ 1) for i in range(8)])
    pieces = lax.all_to_all(pieces, "z", 0, 0, tiled=True)
    gated = convolve(lax.all_gather(pieces, "core", axis=0), filters, skip.reshape(1, -1), 4)
    others = [lax.ppermute(rows, "core", [(0, 1), (1, 0)]) for rows in (own, beside)]
    shape = gated.shape
    gated = lax.all_to_all(gated.reshape((-1,) + shape[2:]), ("y_far", "z"), 0, 0, tiled=True)
    parts = mix(gated.reshape(shape), own, beside, *others)
    return add(lax.all_to_all(parts, near, 0, 0, tiled=True))


def solution(mesh):
    fine = Mesh(mesh.devices.reshape(8, 2, 4, 4, 2), ("z", "core", "x", "y_far", "y_near"))
    seq, chan = ("z", "core"), ("x", "y_far", "y_near")
    in_specs = (P(seq, chan), P(None, None, chan), P(chan, None), P(chan), P(None, chan))
    return jax.shard_map(shards, mesh=fine, in_specs=in_specs, out_specs=P(seq, chan), check_vma=False)
```

```python
import jax
import jax.numpy as jnp
from jax import lax
from jax.experimental import pallas as pl
from jax.experimental.pallas import tpu as pltpu
from jax.sharding import Mesh
from jax.sharding import PartitionSpec as P

GROUP = 16
LANES = 128
PARAMS = pltpu.CompilerParams(vmem_limit_bytes=40 * 2**20)


def vmem(*shape_and_map):
    return pl.BlockSpec(*shape_and_map, memory_space=pltpu.VMEM)


def pack_kernel(x_ref, w_hbm, out_ref, sems):
    far, tokens, _ = x_ref.shape
    depth = w_hbm.shape[1]
    mine = 2 * lax.axis_index("core") + lax.rem(lax.axis_index("z"), 2)
    sends = [
        pltpu.make_async_copy(
            w_hbm.at[(peer // 2 * far + mine) * 2 + peer % 2],
            out_ref.at[peer, pl.ds(far * tokens, depth)],
            sems.at[peer],
        )
        for peer in range(out_ref.shape[0])
    ]
    for send in sends:
        send.start()
    x = x_ref[...].reshape(far * tokens, -1)
    for peer in range(out_ref.shape[0]):
        out_ref[peer, : far * tokens] = x
    for send in sends:
        send.wait()


def pack(x, w, peers):
    far, tokens, depth = x.shape
    w = pltpu.with_memory_space_constraint(w.reshape(-1, depth, w.shape[1]), pltpu.HBM)
    return pl.pallas_call(
        pack_kernel,
        in_specs=[vmem(), pl.BlockSpec(memory_space=pltpu.HBM)],
        out_specs=vmem(),
        out_shape=jax.ShapeDtypeStruct((peers, far * tokens + depth, depth), x.dtype),
        scratch_shapes=[pltpu.SemaphoreType.DMA((peers,))],
        compiler_params=PARAMS,
        name="pack",
    )(x, w)


def project_kernel(x_ref, w_ref, out_ref, rows_ref):
    depth, chans = x_ref.shape[2], w_ref.shape[2]
    tokens = out_ref.shape[2]
    far = w_ref.shape[1] // (x_ref.shape[0] * depth)
    span = 2 * far * depth
    rows_ref[...] = x_ref[:, far * tokens :]
    acc = None
    for step in range(x_ref.shape[0] // 2):
        left = jnp.concatenate(
            [x_ref[2 * step + j, i * tokens : (i + 1) * tokens] for i in range(far) for j in range(2)], axis=1
        )
        right = jnp.concatenate([w_ref[i, step * span : (step + 1) * span] for i in range(3)], axis=1)
        part = jnp.dot(left, right, preferred_element_type=jnp.float32)
        acc = part if acc is None else acc + part
    query, key, value = (
        acc[:, i * chans : (i + 1) * chans].astype(jnp.bfloat16).astype(jnp.float32) for i in range(3)
    )
    groups = chans // GROUP
    out_ref[:, :GROUP, :] = (key * value).T.astype(jnp.bfloat16).reshape(groups, GROUP, -1)
    out_ref[:, GROUP:, :] = query.T.astype(jnp.bfloat16).reshape(groups, GROUP, -1)


def project(x, w, tokens):
    chans = w.shape[2]
    rows = x.shape[1] - w.shape[1] // (x.shape[0] * x.shape[2]) * tokens
    return pl.pallas_call(
        project_kernel,
        in_specs=[vmem(), vmem()],
        out_specs=[vmem(), vmem()],
        out_shape=[
            jax.ShapeDtypeStruct((chans // GROUP, 2 * GROUP, tokens), jnp.bfloat16),
            jax.ShapeDtypeStruct((x.shape[0], rows, x.shape[2]), jnp.bfloat16),
        ],
        compiler_params=PARAMS,
        name="project",
    )(x, w)


def conv_kernel(pieces_ref, filters_ref, skip_ref, out_ref, shifted_ref, strip_ref, skip_rows_ref, acc_ref):
    core, group = lax.axis_index("core"), lax.axis_index("z")
    blocks, _, block = pieces_ref.shape[1:]
    rows = blocks * GROUP
    own = pieces_ref[core]
    source = own[:, :GROUP, :].reshape(rows, block)
    query = own[:, GROUP:, :].reshape(rows, block)
    other = pieces_ref[1 - core][:, :GROUP, :].reshape(rows, block)
    shifted_ref[:GROUP, :] = jnp.zeros((GROUP, block), jnp.bfloat16)
    shifted_ref[GROUP:, :] = other
    other = shifted_ref[pl.ds(pl.multiple_of(core * GROUP, GROUP), rows), :]
    left = jnp.concatenate([source, other], axis=1)

    all_taps = filters_ref[...].astype(jnp.float32)
    mine = lax.broadcasted_iota(jnp.int32, all_taps.shape, 0) == group
    taps = jnp.sum(jnp.where(mine, all_taps, 0.0), axis=0, keepdims=True)
    length = taps.shape[1]
    padded = jnp.concatenate([jnp.zeros((1, LANES), jnp.float32), taps], axis=1)
    rolled = pltpu.roll(jnp.broadcast_to(padded, (LANES, LANES + length)), 0, 1, stride=1, stride_axis=0)
    strip_ref[:, :LANES] = jnp.zeros((LANES, LANES), jnp.bfloat16)
    strip_ref[:, LANES:] = rolled[:, LANES:].astype(jnp.bfloat16)

    for e in range(blocks):
        first = 2 * e * block
        right = jnp.concatenate(
            [
                strip_ref[:, at : at + block]
                for at in (first + LANES, first, first + block + LANES, first + block)
            ],
            axis=0,
        )
        height = rows - e * GROUP
        part = jnp.dot(left[:height], right, preferred_element_type=jnp.float32)
        if e == 0:
            acc_ref[...] = part
        else:
            acc_ref[e * GROUP :, :] += part

    skip_rows_ref[...] = jnp.broadcast_to(skip_ref[...], (LANES, LANES)).T
    skip = skip_rows_ref[pl.ds(pl.multiple_of(group * GROUP, GROUP), GROUP), :]
    skip = jnp.concatenate([skip] * (block // LANES), axis=1)
    skip = jnp.concatenate([skip] * blocks, axis=0)
    gated = query.astype(jnp.float32) * (acc_ref[...] + skip * source.astype(jnp.float32))
    gated = gated.astype(jnp.bfloat16).reshape(out_ref.shape[:1] + out_ref.shape[2:])
    for i in range(out_ref.shape[1]):
        out_ref[:, i] = gated


def convolve(pieces, filters, skip, count):
    _, blocks, _, block = pieces.shape
    rows = blocks * GROUP
    return pl.pallas_call(
        conv_kernel,
        in_specs=[vmem(), vmem(), vmem()],
        out_specs=vmem(),
        out_shape=jax.ShapeDtypeStruct((blocks, count, GROUP, block), jnp.bfloat16),
        scratch_shapes=[
            pltpu.VMEM((rows + GROUP, block), jnp.bfloat16),
            pltpu.VMEM((LANES, LANES + filters.shape[1]), jnp.bfloat16),
            pltpu.VMEM((LANES, LANES), jnp.float32),
            pltpu.VMEM((rows, block), jnp.float32),
        ],
        compiler_params=PARAMS,
        name="convolve",
    )(pieces, filters, skip)


def mix_kernel(g_ref, *refs):
    w_refs, out_ref, turned_ref = refs[:-2], refs[-2], refs[-1]
    core, odd = lax.axis_index("core"), lax.rem(lax.axis_index("z"), 2)
    _, far, _, tokens = g_ref.shape
    peers, _, chans = w_refs[0].shape
    for i in range(far):
        turned_ref[i] = g_ref[:, i].astype(jnp.float32).reshape(-1, tokens).T.astype(jnp.bfloat16)
    acc = None
    for pair, at in ((w_refs[:2], core), (w_refs[2:], 1 - core)):
        left = jnp.concatenate([turned_ref[2 * at + odd], turned_ref[2 * at + 1 - odd]], axis=1)
        right = jnp.concatenate(
            [jnp.concatenate([w_ref[peer] for w_ref in pair], axis=0) for peer in range(peers)], axis=1
        )
        part = jnp.dot(left, right, preferred_element_type=jnp.float32)
        acc = part if acc is None else acc + part
    for peer in range(peers):
        out_ref[peer] = acc[:, peer * chans : (peer + 1) * chans].astype(jnp.bfloat16)


def mix(gated, *w):
    groups, far, rows, tokens = gated.shape
    peers, _, chans = w[0].shape
    return pl.pallas_call(
        mix_kernel,
        in_specs=[vmem()] * (1 + len(w)),
        out_specs=vmem(),
        out_shape=jax.ShapeDtypeStruct((peers, tokens, chans), jnp.bfloat16),
        scratch_shapes=[pltpu.VMEM((far, tokens, groups * rows), jnp.bfloat16)],
        compiler_params=PARAMS,
        name="mix",
    )(gated, *w)


def add_kernel(parts_ref, out_ref):
    total = parts_ref[0].astype(jnp.float32)
    for i in range(1, parts_ref.shape[0]):
        total += parts_ref[i].astype(jnp.float32)
    out_ref[...] = total.astype(jnp.bfloat16)


def add(parts):
    return pl.pallas_call(
        add_kernel,
        in_specs=[vmem()],
        out_specs=vmem(),
        out_shape=jax.ShapeDtypeStruct(parts.shape[1:], jnp.bfloat16),
        compiler_params=PARAMS,
        name="add",
    )(parts)


def shards(tokens, w_in, filters, skip, w_out):
    near = ("x", "y_near")
    x = lax.all_gather(tokens, "y_far", axis=0)
    x = lax.all_to_all(pack(x, w_out, 8), near, 0, 0, tiled=True)
    pieces, own = project(x, w_in.transpose(1, 0, 2), tokens.shape[0])
    beside = lax.ppermute(own, "z", [(i, i ^ 1) for i in range(8)])
    pieces = lax.all_to_all(pieces, "z", 0, 0, tiled=True)
    gated = convolve(lax.all_gather(pieces, "core", axis=0), filters, skip.reshape(1, -1), 4)
    others = [lax.ppermute(rows, "core", [(0, 1), (1, 0)]) for rows in (own, beside)]
    shape = gated.shape
    gated = lax.all_to_all(gated.reshape((-1,) + shape[2:]), ("z", "y_far"), 0, 0, tiled=True)
    parts = mix(gated.reshape(shape), own, beside, *others)
    return add(lax.all_to_all(parts, near, 0, 0, tiled=True))


def solution(mesh):
    fine = Mesh(mesh.devices.reshape(8, 2, 4, 4, 2), ("z", "core", "x", "y_far", "y_near"))
    seq, chan = ("z", "core"), ("x", "y_far", "y_near")
    in_specs = (P(seq, chan), P(None, None, chan), P(chan, None), P(chan), P(None, chan))
    return jax.shard_map(shards, mesh=fine, in_specs=in_specs, out_specs=P(seq, chan), check_vma=False)
```

```python
import jax
import jax.numpy as jnp
from jax import lax
from jax.experimental import pallas as pl
from jax.experimental.pallas import tpu as pltpu
from jax.sharding import Mesh
from jax.sharding import PartitionSpec as P

GROUP = 16
LANES = 128
PARAMS = pltpu.CompilerParams(vmem_limit_bytes=40 * 2**20)


def vmem(*shape_and_map):
    return pl.BlockSpec(*shape_and_map, memory_space=pltpu.VMEM)


def pack_kernel(x_ref, w_hbm, out_ref, sem):
    far, tokens, _ = x_ref.shape
    steps, near, rows, _ = out_ref.shape
    mine = 2 * lax.axis_index("core") + lax.rem(lax.axis_index("z"), 2)
    below = out_ref.at[:, :, pl.ds(far * tokens, rows - far * tokens)]
    send = pltpu.make_async_copy(w_hbm.at[:, mine], below, sem)
    send.start()
    x = x_ref[...].reshape(far * tokens, -1)
    for step in range(steps):
        for j in range(near):
            out_ref[step, j, : far * tokens] = x
    send.wait()


def pack(x, w, peers):
    far, tokens, depth = x.shape
    chans = w.shape[1]
    w = pltpu.with_memory_space_constraint(w.reshape(peers // 2, far, 2, depth, chans), pltpu.HBM)
    packed = pl.pallas_call(
        pack_kernel,
        in_specs=[vmem(), pl.BlockSpec(memory_space=pltpu.HBM)],
        out_specs=vmem(),
        out_shape=jax.ShapeDtypeStruct((peers // 2, 2, far * tokens + depth, depth), x.dtype),
        scratch_shapes=[pltpu.SemaphoreType.DMA],
        compiler_params=PARAMS,
        name="pack",
    )(x, w)
    return packed.reshape((peers,) + packed.shape[2:])


def project_kernel(x_ref, w_ref, out_ref, rows_ref):
    depth, chans = x_ref.shape[2], w_ref.shape[2]
    tokens = out_ref.shape[2]
    far = w_ref.shape[1] // (x_ref.shape[0] * depth)
    span = 2 * far * depth
    rows_ref[...] = x_ref[:, far * tokens :]
    acc = None
    for step in range(x_ref.shape[0] // 2):
        left = jnp.concatenate(
            [x_ref[2 * step + j, i * tokens : (i + 1) * tokens] for i in range(far) for j in range(2)], axis=1
        )
        right = jnp.concatenate([w_ref[i, step * span : (step + 1) * span] for i in range(3)], axis=1)
        part = jnp.dot(left, right, preferred_element_type=jnp.float32)
        acc = part if acc is None else acc + part
    query, key, value = (
        acc[:, i * chans : (i + 1) * chans].astype(jnp.bfloat16).astype(jnp.float32) for i in range(3)
    )
    groups = chans // GROUP
    out_ref[:, :GROUP, :] = (key * value).T.astype(jnp.bfloat16).reshape(groups, GROUP, -1)
    out_ref[:, GROUP:, :] = query.T.astype(jnp.bfloat16).reshape(groups, GROUP, -1)


def project(x, w, tokens):
    chans = w.shape[2]
    rows = x.shape[1] - w.shape[1] // (x.shape[0] * x.shape[2]) * tokens
    return pl.pallas_call(
        project_kernel,
        in_specs=[vmem(), vmem()],
        out_specs=[vmem(), vmem()],
        out_shape=[
            jax.ShapeDtypeStruct((chans // GROUP, 2 * GROUP, tokens), jnp.bfloat16),
            jax.ShapeDtypeStruct((x.shape[0], rows, x.shape[2]), jnp.bfloat16),
        ],
        compiler_params=PARAMS,
        name="project",
    )(x, w)


def conv_kernel(pieces_ref, filters_ref, skip_ref, out_ref, shifted_ref, strip_ref, skip_rows_ref, acc_ref):
    core, group = lax.axis_index("core"), lax.axis_index("z")
    blocks, _, block = pieces_ref.shape[1:]
    rows = blocks * GROUP
    own = pieces_ref[core]
    source = own[:, :GROUP, :].reshape(rows, block)
    query = own[:, GROUP:, :].reshape(rows, block)
    other = pieces_ref[1 - core][:, :GROUP, :].reshape(rows, block)
    shifted_ref[:GROUP, :] = jnp.zeros((GROUP, block), jnp.bfloat16)
    shifted_ref[GROUP:, :] = other
    other = shifted_ref[pl.ds(pl.multiple_of(core * GROUP, GROUP), rows), :]
    left = jnp.concatenate([source, other], axis=1)

    all_taps = filters_ref[...].astype(jnp.float32)
    mine = lax.broadcasted_iota(jnp.int32, all_taps.shape, 0) == group
    taps = jnp.sum(jnp.where(mine, all_taps, 0.0), axis=0, keepdims=True)
    length = taps.shape[1]
    padded = jnp.concatenate([jnp.zeros((1, LANES), jnp.float32), taps], axis=1)
    rolled = pltpu.roll(jnp.broadcast_to(padded, (LANES, LANES + length)), 0, 1, stride=1, stride_axis=0)
    strip_ref[:, :LANES] = jnp.zeros((LANES, LANES), jnp.bfloat16)
    strip_ref[:, LANES:] = rolled[:, LANES:].astype(jnp.bfloat16)

    for e in range(blocks):
        first = 2 * e * block
        right = jnp.concatenate(
            [
                strip_ref[:, at : at + block]
                for at in (first + LANES, first, first + block + LANES, first + block)
            ],
            axis=0,
        )
        height = rows - e * GROUP
        part = jnp.dot(left[:height], right, preferred_element_type=jnp.float32)
        if e == 0:
            acc_ref[...] = part
        else:
            acc_ref[e * GROUP :, :] += part

    skip_rows_ref[...] = jnp.broadcast_to(skip_ref[...], (LANES, LANES)).T
    skip = skip_rows_ref[pl.ds(pl.multiple_of(group * GROUP, GROUP), GROUP), :]
    skip = jnp.concatenate([skip] * (block // LANES), axis=1)
    skip = jnp.concatenate([skip] * blocks, axis=0)
    gated = query.astype(jnp.float32) * (acc_ref[...] + skip * source.astype(jnp.float32))
    gated = gated.astype(jnp.bfloat16).reshape(out_ref.shape[1:])
    for i in range(out_ref.shape[0]):
        out_ref[i] = gated


def convolve(pieces, filters, skip, count):
    _, blocks, _, block = pieces.shape
    rows = blocks * GROUP
    return pl.pallas_call(
        conv_kernel,
        in_specs=[vmem(), vmem(), vmem()],
        out_specs=vmem(),
        out_shape=jax.ShapeDtypeStruct((count, blocks, GROUP, block), jnp.bfloat16),
        scratch_shapes=[
            pltpu.VMEM((rows + GROUP, block), jnp.bfloat16),
            pltpu.VMEM((LANES, LANES + filters.shape[1]), jnp.bfloat16),
            pltpu.VMEM((LANES, LANES), jnp.float32),
            pltpu.VMEM((rows, block), jnp.float32),
        ],
        compiler_params=PARAMS,
        name="convolve",
    )(pieces, filters, skip)


def mix_kernel(g_ref, *refs):
    w_refs, out_ref, turned_ref = refs[:-2], refs[-2], refs[-1]
    core, odd = lax.axis_index("core"), lax.rem(lax.axis_index("z"), 2)
    far, _, _, tokens = g_ref.shape
    peers, _, chans = w_refs[0].shape
    for i in range(far):
        turned_ref[i] = g_ref[i].astype(jnp.float32).reshape(-1, tokens).T.astype(jnp.bfloat16)
    acc = None
    for pair, at in ((w_refs[:2], core), (w_refs[2:], 1 - core)):
        left = jnp.concatenate([turned_ref[2 * at + odd], turned_ref[2 * at + 1 - odd]], axis=1)
        right = jnp.concatenate(
            [jnp.concatenate([w_ref[peer] for w_ref in pair], axis=0) for peer in range(peers)], axis=1
        )
        part = jnp.dot(left, right, preferred_element_type=jnp.float32)
        acc = part if acc is None else acc + part
    for peer in range(peers):
        out_ref[peer] = acc[:, peer * chans : (peer + 1) * chans].astype(jnp.bfloat16)


def mix(gated, *w):
    far, groups, rows, tokens = gated.shape
    peers, _, chans = w[0].shape
    return pl.pallas_call(
        mix_kernel,
        in_specs=[vmem()] * (1 + len(w)),
        out_specs=vmem(),
        out_shape=jax.ShapeDtypeStruct((peers, tokens, chans), jnp.bfloat16),
        scratch_shapes=[pltpu.VMEM((far, tokens, groups * rows), jnp.bfloat16)],
        compiler_params=PARAMS,
        name="mix",
    )(gated, *w)


def add_kernel(parts_ref, out_ref):
    total = parts_ref[0].astype(jnp.float32)
    for i in range(1, parts_ref.shape[0]):
        total += parts_ref[i].astype(jnp.float32)
    out_ref[...] = total.astype(jnp.bfloat16)


def add(parts):
    return pl.pallas_call(
        add_kernel,
        in_specs=[vmem()],
        out_specs=vmem(),
        out_shape=jax.ShapeDtypeStruct(parts.shape[1:], jnp.bfloat16),
        compiler_params=PARAMS,
        name="add",
    )(parts)


def shards(tokens, w_in, filters, skip, w_out):
    near = ("x", "y_near")
    x = lax.all_gather(tokens, "y_far", axis=0)
    x = lax.all_to_all(pack(x, w_out, 8), near, 0, 0, tiled=True)
    pieces, own = project(x, w_in.transpose(1, 0, 2), tokens.shape[0])
    beside = lax.ppermute(own, "z", [(i, i ^ 1) for i in range(8)])
    pieces = lax.all_to_all(pieces, "z", 0, 0, tiled=True)
    gated = convolve(lax.all_gather(pieces, "core", axis=0), filters, skip.reshape(1, -1), 4)
    others = [lax.ppermute(rows, "core", [(0, 1), (1, 0)]) for rows in (own, beside)]
    shape = gated.shape
    gated = lax.all_to_all(gated.reshape((-1,) + shape[2:]), ("y_far", "z"), 0, 0, tiled=True)
    parts = mix(gated.reshape(shape), own, beside, *others)
    return add(lax.all_to_all(parts, near, 0, 0, tiled=True))


def solution(mesh):
    fine = Mesh(mesh.devices.reshape(8, 2, 4, 4, 2), ("z", "core", "x", "y_far", "y_near"))
    seq, chan = ("z", "core"), ("x", "y_far", "y_near")
    in_specs = (P(seq, chan), P(None, None, chan), P(chan, None), P(chan), P(None, chan))
    return jax.shard_map(shards, mesh=fine, in_specs=in_specs, out_specs=P(seq, chan), check_vma=False)
```
